128 devices in a mesh: occ: 16 (over y, z), vir: 8 (over x, core).
Axes of the slice: x: 4, y: 4, z: 4, core: 2. Of those that a mesh axis runs over, the one named last changes fastest.
Arguments:
- amplitudes: bfloat16 [256, 8, 64, 4096], P(('occ', 'vir')), may hold values from -6 to 6
- tile_counts: int32 [256], P(('occ', 'vir')), may hold values from 1 to 8, 1536 in all
- tile_owner: int32 [256, 8], P(('occ', 'vir')), may hold values from 0 to 15, all different within a row; in each aligned block of 2 rows (0 to 1, 2 to 3, ...) at most 2 rows name the same one
- tile_local: int32 [256, 8], P(('occ', 'vir')), may hold values from 0 to 15
- pair_map: int32 [256], replicated, may hold values from 0 to 255, each once
- hole_weight: bfloat16 [256, 64, 64], P(('occ', 'vir')), may hold values from -0.75 to 0.75
- fock_tiles: bfloat16 [16, 64, 64], replicated, may hold values from -0.75 to 0.75
- ladder_panels: bfloat16 [256, 4096, 128], P('occ', 'vir'), may hold values from -0.03125 to 0.03125
Outputs:
- local_residual: bfloat16 [256, 8, 64, 4096], P(('occ', 'vir'))
- ladder_panel: bfloat16 [256, 64, 128], P(('occ', 'vir'))
The draws below stay inside these ranges and needn't reach their ends.
Inputs may be any that keep to these rules, and one draw needn't show every extreme that they name: `tile_counts`: entries of a list at or past its count are not used. `tile_owner`: the 8 entries of a pair tile name different owners; among the pair tiles of one device no owner is named by more than 2 entries. `pair_map`: every virtual tile pair stands at exactly one owner position.
All inputs are finite; a program needn't handle non-finite values. No bound on the sum of `tile_counts` on one device may be relied on, other than what follows from the above.
Results may differ from the reference program's by a relative error of at most 0.001.
Values may be sent and summed in bfloat16 or wider, within the bound.
A program may use at most 320 MiB of HBM per device.

```python
import math
import jax
import jax.numpy as jnp
import numpy as np
from jax import lax

VT = 64
NVT = 16
OPT = 64
SLOTS = 8
PT_DEV = 2
CAP = 2
PANEL = 128
NTILES = 256
TILE_SZ = 4096
OWNERS = 16
TILE_OWN = 16
PTILES = 256


def place_ends(array, own_key, least, largest):
    longest = array.shape.index(max(array.shape))
    spots = []
    for shift in (0, 1):
        where = [jax.random.randint(jax.random.fold_in(own_key, axis), (), 0, length) for axis, length in enumerate(array.shape)]
        where[longest] = (where[longest] + shift) % array.shape[longest]
        spots.append(tuple(where))
    return array.at[spots[0]].set(least).at[spots[1]].set(largest)


def shard_levels(rng, dims, shards, least, top_value):
    gain, own = 1.0, jax.random.fold_in(rng, 6)
    for axis_at, shards_of in shards:
        steps = jnp.exp(jax.random.uniform(jax.random.fold_in(own, axis_at), (shards_of,), jnp.float32, least / len(shards), top_value / len(shards)))
        gain = gain * jnp.repeat(steps, dims[axis_at] // shards_of).reshape([-1 if axis == axis_at else 1 for axis in range(len(dims))])
    return gain


def split_up(number_of, total, most, slope):
    portions = [(1 << 20) // math.isqrt(rank ** slope) + 1 for rank in range(2, number_of + 1)]
    spare, counts = total - most - (number_of - 1), [1] * (number_of - 1)
    while spare > 0:
        candidates = [i for i in range(number_of - 1) if counts[i] < most]
        mass, left = sum([portions[i] for i in candidates]), spare
        for i in candidates:
            more = min(most - counts[i], max(1, left * portions[i] // mass), spare)
            counts[i] = counts[i] + more
            spare = spare - more
    return np.array([most] + counts)


def uneven(own_key, count, total, reach, skew):
    if count == 2:
        one = jax.random.randint(own_key, (), max(1, total - reach), min(reach, total - 1) + 1)
        return jnp.stack([one, total - one])
    tallies = jnp.asarray(split_up(count, total, reach, skew), jnp.int32)
    twos = (count - 1) // 2
    donor, receiver = tallies[1:1 + 2 * twos:2], tallies[2:2 + 2 * twos:2]
    room = jnp.minimum(donor - 1, reach - receiver)
    passed = jax.random.randint(jax.random.fold_in(own_key, 1), (twos,), 0, 1 << 20) % (room + 1)
    tallies = tallies.at[1:1 + 2 * twos:2].set(donor - passed).at[2:2 + 2 * twos:2].set(receiver + passed)
    return tallies[jax.random.permutation(jax.random.fold_in(own_key, 2), count)]


def deal_out(rng, own, number, rows, number_of, top, reach, skew):
    ranking = jax.random.permutation(rng, number_of)
    heavy_load, usual = load_shares(number_of, rows * top, reach, skew, True), load_shares(number_of, rows * top, reach, skew, False)
    places = jnp.arange(number_of)

    def named(sizes, offset_by):
        used = int((sizes > 0).sum())
        fixed = max(1, used // 4)
        shifted = fixed + (places - fixed + offset_by * (used - fixed)) % max(1, number_of - fixed)
        return jnp.zeros((number_of,), jnp.int32).at[ranking[jnp.where(places < fixed, places, shifted)]].set(jnp.asarray(sizes, jnp.int32))

    sizes = jnp.where(number % 4 == 0, named(heavy_load, number // 4), named(usual, number - number // 4 - 1))
    mixed = jax.random.permutation(jax.random.fold_in(own, 3), number_of)
    source_of, sink = mixed[0:number_of // 2 * 2:2], mixed[1:number_of // 2 * 2:2]
    margin = jnp.minimum(sizes[source_of] - 1, reach - sizes[sink]) // 2
    margin = jnp.where((source_of == ranking[0]) | (sink == ranking[0]) | (sizes[sink] == 0), 0, jnp.maximum(margin, 0))
    shifted = jax.random.randint(jax.random.fold_in(own, 4), (number_of // 2,), 0, 1 << 20) % (margin + 1)
    sizes = sizes.at[source_of].add(-shifted).at[sink].add(shifted)
    members = jnp.searchsorted(jnp.cumsum(sizes), jnp.arange(rows * top), side="right").astype(jnp.int32)
    grid = members.reshape(top, rows).T
    grid = grid[jax.random.permutation(jax.random.fold_in(own, 1), rows)]
    offset_by = jax.random.randint(jax.random.fold_in(own, 2), (rows, 1), 0, top)
    return jnp.take_along_axis(grid, (jnp.arange(top)[None, :] + offset_by) % top, axis=1)


def load_shares(amount, total, most, skew, full):
    portions = [(1 << 20) // math.isqrt(rank ** skew) + 1 for rank in range(1, amount + 1)]
    largest = most if full else min(most, max(-(-total // amount), total * portions[0] // sum(portions)))
    least = 1 if total - largest >= amount - 1 else 0
    given, spare = [largest] + [least] * (amount - 1), total - largest - least * (amount - 1)
    while spare > 0:
        candidates = [i for i in range(1, amount) if given[i] < largest] or [i for i in range(1, amount) if given[i] < most]
        mass, left = sum([portions[i] for i in candidates]), spare
        for i in candidates:
            more = min(most - given[i], max(1, left * portions[i] // mass), spare)
            given[i] = given[i] + more
            spare = spare - more
    return np.array(given)


def centred(own_key, dims, scale, bound, pieces=(), kind=jnp.bfloat16):
    gain = shard_levels(own_key, dims, pieces, -0.22, 0.18) if pieces else 1.0
    values = jax.random.normal(own_key, dims, jnp.float32) * scale * gain
    return jnp.minimum(jnp.maximum(values, -bound), bound).astype(kind)


def setup_inputs(seed: int = 0) -> dict:
    keys = jax.random.split(jax.random.key(seed), 9)
    amplitudes = centred(keys[0], (PTILES, SLOTS, OPT, TILE_SZ), 1.0, 6.0, ((0, 128),))
    tile_counts = uneven(keys[1], PTILES, PTILES * 3 * SLOTS // 4, SLOTS, 1).astype(jnp.int32)
    tile_owner_keys = jax.random.split(jax.random.fold_in(keys[2], 1), PTILES // PT_DEV)
    tile_owner_turns = jax.random.permutation(jax.random.fold_in(keys[2], 3), PTILES // PT_DEV)
    tile_owner = jax.vmap(lambda own, number: deal_out(jax.random.fold_in(keys[2], 2), own, number, PT_DEV, OWNERS, SLOTS, CAP, 2))(tile_owner_keys, tile_owner_turns).reshape((PTILES, SLOTS))
    tile_local = place_ends(jax.random.randint(keys[3], (PTILES, SLOTS), 0, TILE_OWN), jax.random.fold_in(keys[3], 1), 0, TILE_OWN - 1).astype(jnp.int32)
    pair_map = jax.random.permutation(keys[4], NTILES).astype(jnp.int32)
    hole_weight = centred(keys[5], (PTILES, OPT, OPT), OPT ** -0.5, 0.75, ((0, 128),))
    fock_tiles = centred(keys[6], (NVT, VT, VT), VT ** -0.5, 0.75)
    ladder_panels = centred(keys[7], (NTILES, TILE_SZ, PANEL), (TILE_SZ * SLOTS) ** -0.5, 0.03125, ((0, 16), (1, 8)))
    return dict(amplitudes=amplitudes, tile_counts=tile_counts, tile_owner=tile_owner, tile_local=tile_local, pair_map=pair_map, hole_weight=hole_weight, fock_tiles=fock_tiles, ladder_panels=ladder_panels)


def reference(amplitudes, tile_counts, tile_owner, tile_local, pair_map, hole_weight, fock_tiles, ladder_panels):
    tile_pos = (tile_owner * TILE_OWN + tile_local).astype(jnp.int32)
    tile_ident = pair_map[tile_pos].astype(jnp.int32)
    row_tile = (tile_ident // NVT).astype(jnp.int32)
    col_tile = (tile_ident % NVT).astype(jnp.int32)
    used_mask = (jnp.arange(SLOTS, dtype=jnp.int32)[None, :] < tile_counts[:, None]).astype(jnp.float32)
    left_fock = fock_tiles[row_tile].astype(jnp.float32)
    right_fock = fock_tiles[col_tile].astype(jnp.float32)

    def one_tile(inputs):
        blocks, weight, positions, mask_row, left_part, right_part = inputs
        blocks_wide = blocks.astype(jnp.float32)
        hole = jnp.einsum('pq,sqx->spx', weight.astype(jnp.float32), blocks_wide)
        shaped = blocks_wide.reshape(SLOTS, OPT, VT, VT)
        fock_part = jnp.einsum('spce,sed->spcd', shaped, right_part) + jnp.einsum('sce,sped->spcd', left_part, shaped)
        summed = (hole + fock_part.reshape(SLOTS, OPT, TILE_SZ)) * mask_row[:, None, None]
        panels = ladder_panels[positions].astype(jnp.float32)
        ladder = jnp.einsum('spx,sxq->pq', blocks_wide * mask_row[:, None, None], panels)
        return summed.astype(jnp.bfloat16), ladder.astype(jnp.bfloat16)

    local_residual, ladder_panel = lax.map(one_tile, (amplitudes, hole_weight, tile_pos, used_mask, left_fock, right_fock))
    return local_residual, ladder_panel
```

```python
import functools

import jax
import jax.numpy as jnp
from jax import lax
from jax.experimental import pallas as pl
from jax.experimental.pallas import tpu as pltpu
from jax.sharding import PartitionSpec as P

MESH = pl.DeviceIdType.MESH
SIDE = 4
BF16, F32, I32 = jnp.bfloat16, jnp.float32, jnp.int32
HOPS = (1, 3, 2, 0)


def body(
    counts_ref,
    owner_ref,
    local_ref,
    map_ref,
    amp_ref,
    hole_ref,
    fock_ref,
    panel_ref,
    res_ref,
    lad_ref,
    amp_vm,
    out_vm,
    arrived,
    panels,
    meta_vm,
    meta_in,
    meta_sm,
    part,
    part_in,
    ring_sum,
    home_in,
    fock_right,
    fock_left,
    spread,
    turned,
    amp_sem,
    out_sem,
    send_sem,
    arrive_sem,
    meta_send,
    meta_sem,
    panel_send,
    panel_own,
    panel_first,
    panel_second,
    part_send,
    part_sem,
    home_send,
    home_sem,
):
    tiles, slots, rows, width = amp_ref.shape
    per_owner = panel_ref.shape[0]
    side = fock_ref.shape[1]
    cols = 128
    occ, vir = lax.axis_index("occ"), lax.axis_index("vir")
    y, z = occ // SIDE, occ % SIDE
    x, c = vir // 2, vir % 2
    w = jnp.where(c == 0, z, y)
    u = jnp.where(c == 0, y, z)

    def at(xx, ww, uu, core):
        own = jnp.where(core == 0, uu * SIDE + ww, ww * SIDE + uu)
        return (own, xx * 2 + core)

    def ring(v, d):
        return lax.rem(v + d + SIDE, SIDE)

    barrier = pltpu.get_barrier_semaphore()
    greeted = 0
    for dx in range(SIDE):
        for dw in range(SIDE):
            for dc in range(2):
                if (dx, dw, dc) != (0, 0, 0):
                    cc = lax.rem(c + dc, 2)
                    own = jnp.where(c == 0, u * SIDE + ring(w, dw), ring(w, dw) * SIDE + u)
                    pl.semaphore_signal(
                        barrier, inc=1, device_id=(own, ring(x, dx) * 2 + cc), device_id_type=MESH
                    )
                    greeted += 1
    for du in range(1, SIDE):
        pl.semaphore_signal(barrier, inc=1, device_id=at(x, w, ring(u, du), c), device_id_type=MESH)
        greeted += 1

    for k in range(tiles * slots):
        pltpu.make_async_copy(
            amp_ref.at[k // slots, k % slots], amp_vm.at[k], amp_sem.at[k]
        ).start()
    lane = lax.broadcasted_iota(I32, (8, 128), 1)
    row = lax.broadcasted_iota(I32, (8, 128), 0)
    listed = jnp.zeros((8, 128), I32)
    for t in range(tiles):
        for s in range(slots):
            own, loc = owner_ref[t, s], local_ref[t, s]
            used = counts_ref[t] > s
            none = per_owner * SIDE * SIDE
            straight = jnp.where(used, own * per_owner + loc, none)
            crossed = jnp.where(
                used, ((own % SIDE) * SIDE + own // SIDE) * per_owner + loc, none
            )
            here = lane == t * slots + s
            listed = jnp.where(here & (row == 0), straight, listed)
            listed = jnp.where(here & (row == 1), crossed, listed)
    meta_vm[...] = listed
    panels[per_owner * SIDE * SIDE] = jnp.zeros((cols, panel_ref.shape[2]), BF16)

    pl.semaphore_wait(barrier, greeted)

    def my_rows(ww):
        return panel_ref.at[:, pl.ds(pl.multiple_of(ww * cols, cols), cols), :]

    def place(uu, ww):
        return panels.at[pl.ds((uu * SIDE + ww) * per_owner, per_owner)]

    own_panel = pltpu.make_async_copy(my_rows(w), place(u, w), panel_own)
    own_panel.start()
    for dw in (1, 3, 2):
        pltpu.make_async_remote_copy(
            src_ref=my_rows(ring(w, dw)),
            dst_ref=place(u, w),
            send_sem=panel_send,
            recv_sem=panel_first.at[dw],
            device_id=at(x, ring(w, dw), u, c),
            device_id_type=MESH,
        ).start()

    half = slots // 2

    def handler(i):
        dw, h, k = i // 8, (i // 4) % 2, i % 4
        dx = jnp.where(k == 0, HOPS[0], jnp.where(k == 1, HOPS[1], jnp.where(k == 2, HOPS[2], HOPS[3])))
        xx = ring(x, dx)
        ww = ring(jnp.where(h == 0, z, y), dw)
        uu = jnp.where(h == 0, y, z)
        own = (dw == 0) & (dx == 0) & (h == c)
        col = (2 * xx + h) * (SIDE * cols) + ww * cols
        slot = (dw * SIDE + dx) * 2 + c
        return own, at(xx, ww, uu, h), col, slot

    def send_piece(r):
        t, s = r // 2, (r % 2) * half

        def one(i, _):
            own, device, col, slot = handler(i)
            src = amp_ref.at[t, pl.ds(s, half), :, pl.ds(pl.multiple_of(col, cols), cols)]
            dst = arrived.at[slot, t, pl.ds(s, half)]

            @pl.when(own)
            def _():
                pltpu.make_async_copy(src, dst, arrive_sem.at[slot, r]).start()

            @pl.when(jnp.logical_not(own))
            def _():
                pltpu.make_async_remote_copy(
                    src_ref=src,
                    dst_ref=dst,
                    send_sem=send_sem,
                    recv_sem=arrive_sem.at[slot, r],
                    device_id=device,
                    device_id_type=MESH,
                ).start()

            return 0

        lax.fori_loop(0, 32, one, 0)

    def send_meta(i, _):
        own, device, _, slot = handler(i)

        @pl.when(own)
        def _():
            pltpu.make_async_copy(meta_vm, meta_in.at[slot], meta_sem.at[slot]).start()

        @pl.when(jnp.logical_not(own))
        def _():
            pltpu.make_async_remote_copy(
                src_ref=meta_vm,
                dst_ref=meta_in.at[slot],
                send_sem=meta_send,
                recv_sem=meta_sem.at[slot],
                device_id=device,
                device_id_type=MESH,
            ).start()

        return 0

    send_piece(0)
    lax.fori_loop(0, 32, send_meta, 0)

    order = lax.broadcasted_iota(I32, (side, side), 0)
    source = lax.broadcasted_iota(I32, (side, side), 1)
    sort = (source == 2 * (order % (side // 2)) + order // (side // 2)).astype(BF16)
    zero = jnp.zeros((side, side), BF16)

    def prepare(n, _):
        f = fock_ref[n]
        top = jnp.concatenate([f, zero], axis=1)
        low = jnp.concatenate([zero, f], axis=1)
        fock_right[n] = jnp.concatenate([top, low], axis=0)
        g = jnp.dot(sort, f, preferred_element_type=F32).astype(BF16)
        g = lax.dot_general(g, sort, (((1,), (1,)), ((), ())), preferred_element_type=F32)
        fock_left[n] = g.astype(BF16)
        return 0

    lax.fori_loop(0, fock_ref.shape[0], prepare, 0)

    chunks = width // cols
    low_half = lax.broadcasted_iota(I32, (chunks, cols), 1) < side

    def residual(k, _):
        t, s = k // slots, k % slots
        pltpu.make_async_copy(amp_ref.at[t, s], amp_vm.at[k], amp_sem.at[k]).wait()
        ident = map_ref[owner_ref[t, s] * per_owner + local_ref[t, s]]
        used = counts_ref[t] > s
        row_tile = ident // fock_ref.shape[0]
        col_tile = ident % fock_ref.shape[0]
        for j in range(chunks):
            spread[pl.ds(j, rows, stride=chunks), :] = amp_vm[k, :, j * cols : (j + 1) * cols].astype(F32)
        for q in range(rows // 2):
            a = spread[2 * q * chunks : (2 * q + 1) * chunks, :]
            b = spread[(2 * q + 1) * chunks : (2 * q + 2) * chunks, :]
            even = jnp.where(low_half, a, pltpu.roll(b, side, 1))
            odd = jnp.where(low_half, pltpu.roll(a, side, 1), b)
            turned[:, q * cols : (q + 1) * cols] = jnp.concatenate([even, odd], axis=0).astype(BF16)
        left = jnp.dot(fock_left[row_tile], turned[...], preferred_element_type=F32)
        for q in range(rows // 2):
            even = left[:chunks, q * cols : (q + 1) * cols]
            odd = left[chunks:, q * cols : (q + 1) * cols]
            spread[2 * q * chunks : (2 * q + 1) * chunks, :] = jnp.where(
                low_half, even, pltpu.roll(odd, side, 1)
            )
            spread[(2 * q + 1) * chunks : (2 * q + 2) * chunks, :] = jnp.where(
                low_half, pltpu.roll(even, side, 1), odd
            )
        weight = hole_ref[t]
        right = fock_right[col_tile]
        for j in range(chunks):
            block = amp_vm[k, :, j * cols : (j + 1) * cols]
            total = jnp.dot(weight, block, preferred_element_type=F32)
            total += jnp.dot(block, right, preferred_element_type=F32)
            total += spread[pl.ds(j, rows, stride=chunks), :]
            out_vm[k, :, j * cols : (j + 1) * cols] = jnp.where(used, total, 0.0).astype(BF16)
        pltpu.make_async_copy(out_vm.at[k], res_ref.at[t, s], out_sem).start()
        return 0

    def pass_panels(ww):
        for du in (1, 3, 2):
            pltpu.make_async_remote_copy(
                src_ref=place(u, ww),
                dst_ref=place(u, ww),
                send_sem=panel_send,
                recv_sem=panel_second.at[du, ring(ww, SIDE - w)],
                device_id=at(x, w, ring(u, du), c),
                device_id_type=MESH,
            ).start()

    own_panel.wait()
    pass_panels(w)
    for dw in (1, 3, 2):
        there = place(u, ring(w, SIDE - dw))
        pltpu.make_async_copy(there, there, panel_first.at[dw]).wait()
        pass_panels(ring(w, SIDE - dw))
    send_piece(1)
    lax.fori_loop(0, 8, residual, 0)
    send_piece(2)
    send_piece(3)
    lax.fori_loop(8, 16, residual, 0)

    for dw in range(SIDE):
        for du in range(1, SIDE):
            there = place(ring(u, SIDE - du), ring(w, dw))
            pltpu.make_async_copy(there, there, panel_second.at[du, dw]).wait()

    def wait_meta(slot, _):
        pltpu.make_async_copy(meta_vm, meta_in.at[slot], meta_sem.at[slot]).wait()
        return 0

    lax.fori_loop(0, 32, wait_meta, 0)
    pltpu.sync_copy(meta_in, meta_sm)

    def ladder(slot, t, h):
        r = t * 2 + h
        there = arrived.at[slot, t, pl.ds(h * half, half)]
        pltpu.make_async_copy(there, there, arrive_sem.at[slot, r]).wait()
        blocks, weights = [], []
        for s in range(h * half, (h + 1) * half):
            blocks.append(arrived[slot, t, s])
            weights.append(panels[meta_sm[slot, c, t * slots + s]])
        return jnp.dot(
            jnp.concatenate(blocks, axis=1),
            jnp.concatenate(weights, axis=0),
            preferred_element_type=F32,
        )

    def first_half(t):
        def one(slot, _):
            part[t, slot] = ladder(slot, t, 0)
            return 0

        lax.fori_loop(0, 32, one, 0)

    def second_half(t):
        def one(slot, _):
            part[t, slot] += ladder(slot, t, 1)
            return 0

        for dw in (2, 1, 3, 0):
            lax.fori_loop(dw * 8, dw * 8 + 8, one, 0)
            if dw:
                pltpu.make_async_remote_copy(
                    src_ref=part.at[t, pl.ds(dw * 8, 8)],
                    dst_ref=part_in.at[t, dw - 1],
                    send_sem=part_send,
                    recv_sem=part_sem.at[t, dw - 1],
                    device_id=at(x, ring(w, SIDE - dw), u, c),
                    device_id_type=MESH,
                ).start()

    def send_home(t):
        for dw in range(1, SIDE):
            there = part_in.at[t, dw - 1]
            pltpu.make_async_copy(there, there, part_sem.at[t, dw - 1]).wait()
        for k in (2, 3, 6, 7, 4, 5, 0, 1):
            dx, core = k // 2, k % 2
            ring_sum[t, k] = (
                part[t, k] + part_in[t, 0, k] + part_in[t, 1, k] + part_in[t, 2, k]
            )
            src, dst, sem = ring_sum.at[t, k], home_in.at[t, c, dx], home_sem.at[t, c, dx]

            def far(src=src, dst=dst, sem=sem, dx=dx, core=core):
                pltpu.make_async_remote_copy(
                    src_ref=src,
                    dst_ref=dst,
                    send_sem=home_send,
                    recv_sem=sem,
                    device_id=(occ, ring(x, SIDE - dx) * 2 + core),
                    device_id_type=MESH,
                ).start()

            if dx:
                far()
            else:
                pl.when(c != core)(far)

                @pl.when(c == core)
                def _(src=src, dst=dst, sem=sem):
                    pltpu.make_async_copy(src, dst, sem).start()

    def finish(t):
        total = jnp.zeros(lad_ref.shape[1:], F32)
        for h in range(2):
            for dx in range(SIDE):
                there = home_in.at[t, h, dx]
                pltpu.make_async_copy(there, there, home_sem.at[t, h, dx]).wait()
                total = total + home_in[t, h, dx]
        lad_ref[t] = total.astype(BF16)

    first_half(0)
    second_half(0)
    first_half(1)
    send_home(0)
    second_half(1)
    finish(0)
    send_home(1)
    finish(1)

    def drained(ref, sem):
        pltpu.make_async_copy(ref, ref, sem).wait()

    drained(amp_ref.at[:, :, :, pl.ds(0, width - cols)], send_sem)
    drained(meta_in.at[pl.ds(0, 31)], meta_send)
    drained(panels.at[pl.ds(0, 15 * per_owner)], panel_send)
    drained(part_in, part_send)
    drained(home_in.at[:, 0], home_send)
    drained(home_in.at[:, 0, pl.ds(0, 3)], home_send)
    drained(out_vm, out_sem)


def per_device(
    amplitudes,
    tile_counts,
    tile_owner,
    tile_local,
    pair_map,
    hole_weight,
    fock_tiles,
    ladder_panels,
):
    tiles, slots, rows, width = amplitudes.shape
    per_owner, depth, panel = ladder_panels.shape
    tile_count, side, _ = fock_tiles.shape
    cols = 128
    dma = pltpu.SemaphoreType.DMA
    smem, vmem, hbm = (pl.BlockSpec(memory_space=m) for m in (pltpu.SMEM, pltpu.VMEM, pl.ANY))
    flops = 2 * tiles * slots * rows * width * (3 * side + panel)
    return pl.pallas_call(
        body,
        out_shape=(
            jax.ShapeDtypeStruct(amplitudes.shape, BF16),
            jax.ShapeDtypeStruct((tiles, rows, panel), BF16),
        ),
        in_specs=[smem, smem, smem, smem, hbm, vmem, vmem, hbm],
        out_specs=(hbm, vmem),
        scratch_shapes=[
            pltpu.VMEM((tiles * slots, rows, width), BF16),
            pltpu.VMEM((tiles * slots, rows, width), BF16),
            pltpu.VMEM((32, tiles, slots, rows, cols), BF16),
            pltpu.VMEM((16 * per_owner + 1, cols, panel), BF16),
            pltpu.VMEM((8, 128), I32),
            pltpu.VMEM((32, 8, 128), I32),
            pltpu.SMEM((32, 8, 128), I32),
            pltpu.VMEM((tiles, 32, rows, panel), F32),
            pltpu.VMEM((tiles, 3, 8, rows, panel), F32),
            pltpu.VMEM((tiles, 8, rows, panel), F32),
            pltpu.VMEM((tiles, 2, SIDE, rows, panel), F32),
            pltpu.VMEM((tile_count, 2 * side, 2 * side), BF16),
            pltpu.VMEM((tile_count, side, side), BF16),
            pltpu.VMEM((rows * width // cols, cols), F32),
            pltpu.VMEM((side, rows * width // side), BF16),
            dma((tiles * slots,)),
            dma(()),
            dma(()),
            dma((32, 4)),
            dma(()),
            dma((32,)),
            dma(()),
            dma(()),
            dma((SIDE,)),
            dma((SIDE, SIDE)),
            dma(()),
            dma((tiles, 3)),
            dma(()),
            dma((tiles, 2, SIDE)),
        ],
        compiler_params=pltpu.CompilerParams(
            collective_id=0, has_side_effects=True, vmem_limit_bytes=60 << 20
        ),
        cost_estimate=pl.CostEstimate(
            flops=flops, bytes_accessed=4 * tiles * slots * rows * width, transcendentals=0
        ),
    )(
        tile_counts,
        tile_owner,
        tile_local,
        pair_map,
        amplitudes,
        hole_weight,
        fock_tiles,
        ladder_panels,
    )


def solution(mesh):
    in_specs = (
        P(("occ", "vir"), None, None, None),
        P(("occ", "vir")),
        P(("occ", "vir"), None),
        P(("occ", "vir"), None),
        P(),
        P(("occ", "vir"), None, None),
        P(),
        P("occ", "vir", None),
    )
    out_specs = (P(("occ", "vir"), None, None, None), P(("occ", "vir"), None, None))
    return jax.shard_map(
        per_device, mesh=mesh, in_specs=in_specs, out_specs=out_specs, check_vma=False
    )
```

```python
import functools

import jax
import jax.numpy as jnp
from jax import lax
from jax.experimental import pallas as pl
from jax.experimental.pallas import tpu as pltpu
from jax.sharding import PartitionSpec as P

MESH = pl.DeviceIdType.MESH
SIDE = 4
BF16, F32, I32 = jnp.bfloat16, jnp.float32, jnp.int32
HOPS = (1, 3, 2, 0)
RINGS = (2, 1, 3, 0)


def body(
    counts_ref,
    owner_ref,
    local_ref,
    map_ref,
    amp_ref,
    hole_ref,
    fock_ref,
    panel_ref,
    res_ref,
    lad_ref,
    amp_vm,
    arrived,
    panels,
    meta_vm,
    meta_in,
    meta_sm,
    part,
    part_in,
    ring_sum,
    home_in,
    fock_right,
    fock_left,
    spread,
    turned,
    amp_sem,
    send_sem,
    arrive_sem,
    meta_send,
    meta_sem,
    panel_send,
    panel_own,
    panel_first,
    panel_second,
    panel_third,
    part_send,
    part_sem,
    home_send,
    home_sem,
):
    tiles, slots, rows, width = amp_ref.shape
    per_owner = panel_ref.shape[0]
    side = fock_ref.shape[1]
    cols = 128
    occ, vir = lax.axis_index("occ"), lax.axis_index("vir")
    y, z = occ // SIDE, occ % SIDE
    x, c = vir // 2, vir % 2
    w = jnp.where(c == 0, z, y)
    u = jnp.where(c == 0, y, z)

    def at(xx, ww, uu, core):
        own = jnp.where(core == 0, uu * SIDE + ww, ww * SIDE + uu)
        return (own, xx * 2 + core)

    def ring(v, d):
        return lax.rem(v + d + SIDE, SIDE)

    barrier = pltpu.get_barrier_semaphore()
    greeted = 0
    for dx in range(SIDE):
        for dw in range(SIDE):
            for dc in range(2):
                if (dx, dw, dc) != (0, 0, 0):
                    cc = lax.rem(c + dc, 2)
                    own = jnp.where(c == 0, u * SIDE + ring(w, dw), ring(w, dw) * SIDE + u)
                    pl.semaphore_signal(
                        barrier, inc=1, device_id=(own, ring(x, dx) * 2 + cc), device_id_type=MESH
                    )
                    greeted += 1
    for du in range(1, SIDE):
        pl.semaphore_signal(barrier, inc=1, device_id=at(x, w, ring(u, du), c), device_id_type=MESH)
        greeted += 1

    for k in range(tiles * slots):
        pltpu.make_async_copy(
            amp_ref.at[k // slots, k % slots], amp_vm.at[k], amp_sem.at[k]
        ).start()
    lane = lax.broadcasted_iota(I32, (8, 128), 1)
    row = lax.broadcasted_iota(I32, (8, 128), 0)
    listed = jnp.zeros((8, 128), I32)
    for t in range(tiles):
        for s in range(slots):
            own, loc = owner_ref[t, s], local_ref[t, s]
            used = counts_ref[t] > s
            none = per_owner * SIDE * SIDE
            straight = jnp.where(used, own * per_owner + loc, none)
            crossed = jnp.where(
                used, ((own % SIDE) * SIDE + own // SIDE) * per_owner + loc, none
            )
            here = lane == t * slots + s
            listed = jnp.where(here & (row == 0), straight, listed)
            listed = jnp.where(here & (row == 1), crossed, listed)
    meta_vm[...] = listed
    panels[per_owner * SIDE * SIDE] = jnp.zeros((cols, panel_ref.shape[2]), BF16)

    pl.semaphore_wait(barrier, greeted)

    def my_rows(ww):
        return panel_ref.at[:, pl.ds(pl.multiple_of(ww * cols, cols), cols), :]

    def place(uu, ww):
        return panels.at[pl.ds((uu * SIDE + ww) * per_owner, per_owner)]

    own_panel = pltpu.make_async_copy(my_rows(w), place(u, w), panel_own)
    own_panel.start()
    for dw in (1, 3, 2):
        pltpu.make_async_remote_copy(
            src_ref=my_rows(ring(w, dw)),
            dst_ref=place(u, w),
            send_sem=panel_send,
            recv_sem=panel_first.at[dw],
            device_id=at(x, ring(w, dw), u, c),
            device_id_type=MESH,
        ).start()

    part_tiles = per_owner // 2

    def place_part(uu, ww, p):
        return panels.at[pl.ds((uu * SIDE + ww) * per_owner + p * part_tiles, part_tiles)]

    def pass_panels(dw, p, du):
        there = place_part(u, ring(w, dw), p)
        held = panel_ref.at[
            pl.ds(p * part_tiles, part_tiles), pl.ds(pl.multiple_of(w * cols, cols), cols), :
        ]
        pltpu.make_async_remote_copy(
            src_ref=there if dw else held,
            dst_ref=there,
            send_sem=panel_send,
            recv_sem=panel_second.at[dw, p, du // 2],
            device_id=at(x, w, ring(u, du), c),
            device_id_type=MESH,
        ).start()

    def wait_neighbour(dw, p, du):
        there = place_part(ring(u, SIDE - du), ring(w, dw), p)
        pltpu.make_async_copy(there, there, panel_second.at[dw, p, du // 2]).wait()

    def pass_on(dw, p):
        du = 1 if p == 0 else SIDE - 1
        there = place_part(ring(u, SIDE - du), ring(w, dw), p)
        pltpu.make_async_remote_copy(
            src_ref=there,
            dst_ref=there,
            send_sem=panel_send,
            recv_sem=panel_third.at[dw, p],
            device_id=at(x, w, ring(u, du), c),
            device_id_type=MESH,
        ).start()

    def wait_first(dw):
        there = place(u, ring(w, dw))
        pltpu.make_async_copy(there, there, panel_first.at[SIDE - dw]).wait()

    def second(dw):
        if dw:
            wait_first(dw)
        for p, du in ((0, 1), (1, 3), (1, 1), (0, 3)):
            pass_panels(dw, p, du)

    def third(dw):
        wait_neighbour(dw, 0, 1)
        pass_on(dw, 0)
        wait_neighbour(dw, 1, 3)
        pass_on(dw, 1)

    def all_panels():
        own_panel.wait()
        for dw in range(SIDE):
            wait_neighbour(dw, 1, 1)
            wait_neighbour(dw, 0, 3)
            for p in range(2):
                there = place_part(ring(u, 2), ring(w, dw), p)
                pltpu.make_async_copy(there, there, panel_third.at[dw, p]).wait()

    second(0)

    half = slots // 2

    def handler(i):
        def pick(k, table):
            return jnp.where(
                k == 0, table[0], jnp.where(k == 1, table[1], jnp.where(k == 2, table[2], table[3]))
            )

        dw, h, dx = pick(i // 8, RINGS), (i // 4) % 2, pick(i % 4, HOPS)
        xx = ring(x, dx)
        ww = ring(jnp.where(h == 0, z, y), dw)
        uu = jnp.where(h == 0, y, z)
        own = (dw == 0) & (dx == 0) & (h == c)
        col = (2 * xx + h) * (SIDE * cols) + ww * cols
        slot = (dw * SIDE + dx) * 2 + c
        return own, at(xx, ww, uu, h), col, slot

    def send_piece(r, first=0, last=32):
        t, s = r // 2, (r % 2) * half

        def one(i, _):
            own, device, col, slot = handler(i)
            src = amp_ref.at[t, pl.ds(s, half), :, pl.ds(pl.multiple_of(col, cols), cols)]
            dst = arrived.at[slot, t, pl.ds(s, half)]

            @pl.when(own)
            def _():
                pltpu.make_async_copy(src, dst, arrive_sem.at[slot, r]).start()

            @pl.when(jnp.logical_not(own))
            def _():
                pltpu.make_async_remote_copy(
                    src_ref=src,
                    dst_ref=dst,
                    send_sem=send_sem,
                    recv_sem=arrive_sem.at[slot, r],
                    device_id=device,
                    device_id_type=MESH,
                ).start()

            return 0

        lax.fori_loop(first, last, one, 0)

    def send_meta(i, _):
        own, device, _, slot = handler(i)

        @pl.when(own)
        def _():
            pltpu.make_async_copy(meta_vm, meta_in.at[slot], meta_sem.at[slot]).start()

        @pl.when(jnp.logical_not(own))
        def _():
            pltpu.make_async_remote_copy(
                src_ref=meta_vm,
                dst_ref=meta_in.at[slot],
                send_sem=meta_send,
                recv_sem=meta_sem.at[slot],
                device_id=device,
                device_id_type=MESH,
            ).start()

        return 0

    send_piece(0)
    lax.fori_loop(0, 32, send_meta, 0)

    order = lax.broadcasted_iota(I32, (side, side), 0)
    source = lax.broadcasted_iota(I32, (side, side), 1)
    sort = (source == 2 * (order % (side // 2)) + order // (side // 2)).astype(BF16)
    zero = jnp.zeros((side, side), BF16)

    def prepare(n, _):
        f = fock_ref[n]
        top = jnp.concatenate([f, zero], axis=1)
        low = jnp.concatenate([zero, f], axis=1)
        fock_right[n] = jnp.concatenate([top, low], axis=0)
        g = jnp.dot(sort, f, preferred_element_type=F32).astype(BF16)
        g = lax.dot_general(g, sort, (((1,), (1,)), ((), ())), preferred_element_type=F32)
        fock_left[n] = g.astype(BF16)
        return 0

    lax.fori_loop(0, fock_ref.shape[0], prepare, 0)

    chunks = width // cols
    low_half = lax.broadcasted_iota(I32, (chunks, cols), 1) < side

    def residual(k, _):
        t, s = k // slots, k % slots
        pltpu.make_async_copy(amp_ref.at[t, s], amp_vm.at[k], amp_sem.at[k]).wait()
        ident = map_ref[owner_ref[t, s] * per_owner + local_ref[t, s]]
        used = counts_ref[t] > s
        row_tile = ident // fock_ref.shape[0]
        col_tile = ident % fock_ref.shape[0]
        for j in range(chunks):
            spread[pl.ds(j, rows, stride=chunks), :] = amp_vm[k, :, j * cols : (j + 1) * cols].astype(F32)
        for q in range(rows // 2):
            a = spread[2 * q * chunks : (2 * q + 1) * chunks, :]
            b = spread[(2 * q + 1) * chunks : (2 * q + 2) * chunks, :]
            even = jnp.where(low_half, a, pltpu.roll(b, side, 1))
            odd = jnp.where(low_half, pltpu.roll(a, side, 1), b)
            turned[:, q * cols : (q + 1) * cols] = jnp.concatenate([even, odd], axis=0).astype(BF16)
        left = jnp.dot(fock_left[row_tile], turned[...], preferred_element_type=F32)
        for q in range(rows // 2):
            even = left[:chunks, q * cols : (q + 1) * cols]
            odd = left[chunks:, q * cols : (q + 1) * cols]
            spread[2 * q * chunks : (2 * q + 1) * chunks, :] = jnp.where(
                low_half, even, pltpu.roll(odd, side, 1)
            )
            spread[(2 * q + 1) * chunks : (2 * q + 2) * chunks, :] = jnp.where(
                low_half, pltpu.roll(even, side, 1), odd
            )
        weight = hole_ref[t]
        right = fock_right[col_tile]
        for j in range(chunks):
            block = amp_vm[k, :, j * cols : (j + 1) * cols]
            total = jnp.dot(weight, block, preferred_element_type=F32)
            total += jnp.dot(block, right, preferred_element_type=F32)
            total += spread[pl.ds(j, rows, stride=chunks), :]
            res_ref[t, s, :, j * cols : (j + 1) * cols] = jnp.where(used, total, 0.0).astype(BF16)
        return 0

    lax.fori_loop(0, 2, residual, 0)
    third(0)
    for dw in (3, 1, 2):
        second(dw)
    send_piece(1)
    lax.fori_loop(2, 9, residual, 0)
    for dw in (3, 1, 2):
        third(dw)
    send_piece(2)
    lax.fori_loop(9, 13, residual, 0)
    send_piece(3)
    lax.fori_loop(13, 16, residual, 0)
    all_panels()
    def wait_meta(slot, _):
        pltpu.make_async_copy(meta_vm, meta_in.at[slot], meta_sem.at[slot]).wait()
        return 0

    lax.fori_loop(0, 32, wait_meta, 0)
    pltpu.sync_copy(meta_in, meta_sm)

    def ladder(slot, t, h):
        r = t * 2 + h
        there = arrived.at[slot, t, pl.ds(h * half, half)]
        pltpu.make_async_copy(there, there, arrive_sem.at[slot, r]).wait()
        blocks, weights = [], []
        for s in range(h * half, (h + 1) * half):
            blocks.append(arrived[slot, t, s])
            weights.append(panels[meta_sm[slot, c, t * slots + s]])
        return jnp.dot(
            jnp.concatenate(blocks, axis=1),
            jnp.concatenate(weights, axis=0),
            preferred_element_type=F32,
        )

    def first_half(t):
        def one(slot, _):
            part[t, slot] = ladder(slot, t, 0)
            return 0

        lax.fori_loop(0, 32, one, 0)

    def second_half(t):
        def one(slot, _):
            part[t, slot] += ladder(slot, t, 1)
            return 0

        for dw in RINGS:
            lax.fori_loop(dw * 8, dw * 8 + 8, one, 0)
            if dw:
                pltpu.make_async_remote_copy(
                    src_ref=part.at[t, pl.ds(dw * 8, 8)],
                    dst_ref=part_in.at[t, dw - 1],
                    send_sem=part_send,
                    recv_sem=part_sem.at[t, dw - 1],
                    device_id=at(x, ring(w, SIDE - dw), u, c),
                    device_id_type=MESH,
                ).start()

    def send_home(t):
        for dw in range(1, SIDE):
            there = part_in.at[t, dw - 1]
            pltpu.make_async_copy(there, there, part_sem.at[t, dw - 1]).wait()
        for k in (2, 3, 6, 7, 4, 5, 0, 1):
            dx, core = k // 2, k % 2
            ring_sum[t, k] = (
                part[t, k] + part_in[t, 0, k] + part_in[t, 1, k] + part_in[t, 2, k]
            )
            src, dst, sem = ring_sum.at[t, k], home_in.at[t, c, dx], home_sem.at[t, c, dx]

            def far(src=src, dst=dst, sem=sem, dx=dx, core=core):
                pltpu.make_async_remote_copy(
                    src_ref=src,
                    dst_ref=dst,
                    send_sem=home_send,
                    recv_sem=sem,
                    device_id=(occ, ring(x, SIDE - dx) * 2 + core),
                    device_id_type=MESH,
                ).start()

            if dx:
                far()
            else:
                pl.when(c != core)(far)

                @pl.when(c == core)
                def _(src=src, dst=dst, sem=sem):
                    pltpu.make_async_copy(src, dst, sem).start()

    def finish(t):
        total = jnp.zeros(lad_ref.shape[1:], F32)
        for h in range(2):
            for dx in range(SIDE):
                there = home_in.at[t, h, dx]
                pltpu.make_async_copy(there, there, home_sem.at[t, h, dx]).wait()
                total = total + home_in[t, h, dx]
        lad_ref[t] = total.astype(BF16)

    first_half(0)
    second_half(0)
    first_half(1)
    send_home(0)
    second_half(1)
    finish(0)
    send_home(1)
    finish(1)

    def drained(ref, sem):
        pltpu.make_async_copy(ref, ref, sem).wait()

    drained(amp_ref.at[:, :, :, pl.ds(0, width - cols)], send_sem)
    drained(meta_in.at[pl.ds(0, 31)], meta_send)
    drained(panels.at[pl.ds(0, 15 * per_owner)], panel_send)
    drained(part_in, part_send)
    drained(home_in.at[:, 0], home_send)
    drained(home_in.at[:, 0, pl.ds(0, 3)], home_send)


def per_device(
    amplitudes,
    tile_counts,
    tile_owner,
    tile_local,
    pair_map,
    hole_weight,
    fock_tiles,
    ladder_panels,
):
    tiles, slots, rows, width = amplitudes.shape
    per_owner, depth, panel = ladder_panels.shape
    tile_count, side, _ = fock_tiles.shape
    cols = 128
    dma = pltpu.SemaphoreType.DMA
    smem, vmem, hbm = (pl.BlockSpec(memory_space=m) for m in (pltpu.SMEM, pltpu.VMEM, pl.ANY))
    flops = 2 * tiles * slots * rows * width * (3 * side + panel)
    return pl.pallas_call(
        body,
        out_shape=(
            pltpu.VMEM(amplitudes.shape, BF16),
            jax.ShapeDtypeStruct((tiles, rows, panel), BF16),
        ),
        in_specs=[smem, smem, smem, smem, hbm, vmem, vmem, hbm],
        out_specs=(vmem, vmem),
        scratch_shapes=[
            pltpu.VMEM((tiles * slots, rows, width), BF16),
            pltpu.VMEM((32, tiles, slots, rows, cols), BF16),
            pltpu.VMEM((16 * per_owner + 1, cols, panel), BF16),
            pltpu.VMEM((8, 128), I32),
            pltpu.VMEM((32, 8, 128), I32),
            pltpu.SMEM((32, 8, 128), I32),
            pltpu.VMEM((tiles, 32, rows, panel), F32),
            pltpu.VMEM((tiles, 3, 8, rows, panel), F32),
            pltpu.VMEM((tiles, 8, rows, panel), F32),
            pltpu.VMEM((tiles, 2, SIDE, rows, panel), F32),
            pltpu.VMEM((tile_count, 2 * side, 2 * side), BF16),
            pltpu.VMEM((tile_count, side, side), BF16),
            pltpu.VMEM((rows * width // cols, cols), F32),
            pltpu.VMEM((side, rows * width // side), BF16),
            dma((tiles * slots,)),
            dma(()),
            dma((32, 4)),
            dma(()),
            dma((32,)),
            dma(()),
            dma(()),
            dma((SIDE,)),
            dma((SIDE, 2, 2)),
            dma((SIDE, 2)),
            dma(()),
            dma((tiles, 3)),
            dma(()),
            dma((tiles, 2, SIDE)),
        ],
        compiler_params=pltpu.CompilerParams(
            collective_id=0, has_side_effects=True, vmem_limit_bytes=54 << 20
        ),
        cost_estimate=pl.CostEstimate(
            flops=flops, bytes_accessed=4 * tiles * slots * rows * width, transcendentals=0
        ),
    )(
        tile_counts,
        tile_owner,
        tile_local,
        pair_map,
        amplitudes,
        hole_weight,
        fock_tiles,
        ladder_panels,
    )


def solution(mesh):
    in_specs = (
        P(("occ", "vir"), None, None, None),
        P(("occ", "vir")),
        P(("occ", "vir"), None),
        P(("occ", "vir"), None),
        P(),
        P(("occ", "vir"), None, None),
        P(),
        P("occ", "vir", None),
    )
    out_specs = (P(("occ", "vir"), None, None, None), P(("occ", "vir"), None, None))
    return jax.shard_map(
        per_device, mesh=mesh, in_specs=in_specs, out_specs=out_specs, check_vma=False
    )
```

```python
import functools

import jax
import jax.numpy as jnp
from jax import lax
from jax.experimental import pallas as pl
from jax.experimental.pallas import tpu as pltpu
from jax.sharding import PartitionSpec as P

MESH = pl.DeviceIdType.MESH
SIDE = 4
BF16, F32, I32 = jnp.bfloat16, jnp.float32, jnp.int32
HOPS = (1, 3, 2, 0)
RINGS = (0, 2, 1, 3)


def body(
    counts_ref,
    owner_ref,
    local_ref,
    map_ref,
    amp_ref,
    hole_ref,
    fock_ref,
    panel_ref,
    res_ref,
    lad_ref,
    amp_vm,
    arrived,
    panels,
    meta_vm,
    meta_in,
    meta_sm,
    part,
    part_in,
    ring_sum,
    home_in,
    fock_right,
    fock_left,
    spread,
    turned,
    amp_sem,
    send_sem,
    arrive_sem,
    meta_send,
    meta_sem,
    panel_send,
    panel_own,
    panel_first,
    panel_second,
    panel_third,
    part_send,
    part_sem,
    home_send,
    home_sem,
):
    tiles, slots, rows, width = amp_ref.shape
    per_owner = panel_ref.shape[0]
    side = fock_ref.shape[1]
    cols = 128
    occ, vir = lax.axis_index("occ"), lax.axis_index("vir")
    y, z = occ // SIDE, occ % SIDE
    x, c = vir // 2, vir % 2
    w = jnp.where(c == 0, z, y)
    u = jnp.where(c == 0, y, z)

    def at(xx, ww, uu, core):
        own = jnp.where(core == 0, uu * SIDE + ww, ww * SIDE + uu)
        return (own, xx * 2 + core)

    def pick(k, table):
        return jnp.where(
            k == 0, table[0], jnp.where(k == 1, table[1], jnp.where(k == 2, table[2], table[3]))
        )

    def ring(v, d):
        return lax.rem(v + d + SIDE, SIDE)

    barrier = pltpu.get_barrier_semaphore()
    greeted = 0
    for dx in range(SIDE):
        for dw in range(SIDE):
            for dc in range(2):
                if (dx, dw, dc) != (0, 0, 0):
                    cc = lax.rem(c + dc, 2)
                    own = jnp.where(c == 0, u * SIDE + ring(w, dw), ring(w, dw) * SIDE + u)
                    pl.semaphore_signal(
                        barrier, inc=1, device_id=(own, ring(x, dx) * 2 + cc), device_id_type=MESH
                    )
                    greeted += 1
    for du in range(1, SIDE):
        pl.semaphore_signal(barrier, inc=1, device_id=at(x, w, ring(u, du), c), device_id_type=MESH)
        greeted += 1

    for k in range(tiles * slots):
        pltpu.make_async_copy(
            amp_ref.at[k // slots, k % slots], amp_vm.at[k], amp_sem.at[k]
        ).start()
    lane = lax.broadcasted_iota(I32, (8, 128), 1)
    row = lax.broadcasted_iota(I32, (8, 128), 0)
    listed = jnp.zeros((8, 128), I32)
    for t in range(tiles):
        for s in range(slots):
            own, loc = owner_ref[t, s], local_ref[t, s]
            used = counts_ref[t] > s
            none = per_owner * SIDE * SIDE
            straight = jnp.where(used, own * per_owner + loc, none)
            crossed = jnp.where(
                used, ((own % SIDE) * SIDE + own // SIDE) * per_owner + loc, none
            )
            here = lane == t * slots + s
            listed = jnp.where(here & (row == 0), straight, listed)
            listed = jnp.where(here & (row == 1), crossed, listed)
    meta_vm[...] = listed
    panels[per_owner * SIDE * SIDE] = jnp.zeros((cols, panel_ref.shape[2]), BF16)

    pl.semaphore_wait(barrier, greeted)

    def my_rows(ww):
        return panel_ref.at[:, pl.ds(pl.multiple_of(ww * cols, cols), cols), :]

    def place(uu, ww):
        return panels.at[pl.ds((uu * SIDE + ww) * per_owner, per_owner)]

    own_panel = pltpu.make_async_copy(my_rows(w), place(u, w), panel_own)
    own_panel.start()
    for dw in (1, 3, 2):
        pltpu.make_async_remote_copy(
            src_ref=my_rows(ring(w, dw)),
            dst_ref=place(u, w),
            send_sem=panel_send,
            recv_sem=panel_first.at[dw],
            device_id=at(x, ring(w, dw), u, c),
            device_id_type=MESH,
        ).start()

    part_tiles = per_owner // 2

    def place_part(uu, ww, p):
        return panels.at[pl.ds((uu * SIDE + ww) * per_owner + p * part_tiles, part_tiles)]

    def pass_panels(dw, p, du):
        there = place_part(u, ring(w, dw), p)
        held = panel_ref.at[
            pl.ds(p * part_tiles, part_tiles), pl.ds(pl.multiple_of(w * cols, cols), cols), :
        ]
        pltpu.make_async_remote_copy(
            src_ref=there if dw else held,
            dst_ref=there,
            send_sem=panel_send,
            recv_sem=panel_second.at[dw, p, du // 2],
            device_id=at(x, w, ring(u, du), c),
            device_id_type=MESH,
        ).start()

    def wait_neighbour(dw, p, du):
        there = place_part(ring(u, SIDE - du), ring(w, dw), p)
        pltpu.make_async_copy(there, there, panel_second.at[dw, p, du // 2]).wait()

    def pass_on(dw, p):
        du = 1 if p == 0 else SIDE - 1
        there = place_part(ring(u, SIDE - du), ring(w, dw), p)
        pltpu.make_async_remote_copy(
            src_ref=there,
            dst_ref=there,
            send_sem=panel_send,
            recv_sem=panel_third.at[dw, p],
            device_id=at(x, w, ring(u, du), c),
            device_id_type=MESH,
        ).start()

    def wait_first(dw):
        there = place(u, ring(w, dw))
        pltpu.make_async_copy(there, there, panel_first.at[SIDE - dw]).wait()

    def second(dw):
        if dw:
            wait_first(dw)
        for p, du in ((0, 1), (1, 3), (1, 1), (0, 3)):
            pass_panels(dw, p, du)

    def third(dw):
        wait_neighbour(dw, 0, 1)
        pass_on(dw, 0)
        wait_neighbour(dw, 1, 3)
        pass_on(dw, 1)

    def all_panels():
        own_panel.wait()
        for dw in range(SIDE):
            wait_neighbour(dw, 1, 1)
            wait_neighbour(dw, 0, 3)
            for p in range(2):
                there = place_part(ring(u, 2), ring(w, dw), p)
                pltpu.make_async_copy(there, there, panel_third.at[dw, p]).wait()

    second(0)

    half = slots // 2

    def handler(i):
        dw, h, dx = pick(i // 8, RINGS), (i // 4) % 2, pick(i % 4, HOPS)
        xx = ring(x, dx)
        ww = ring(jnp.where(h == 0, z, y), dw)
        uu = jnp.where(h == 0, y, z)
        own = (dw == 0) & (dx == 0) & (h == c)
        col = (2 * xx + h) * (SIDE * cols) + ww * cols
        slot = (dw * SIDE + dx) * 2 + c
        return own, at(xx, ww, uu, h), col, slot

    def send_piece(r, first=0, last=32):
        t, s = r // 2, (r % 2) * half

        def one(i, _):
            own, device, col, slot = handler(i)
            src = amp_ref.at[t, pl.ds(s, half), :, pl.ds(pl.multiple_of(col, cols), cols)]
            dst = arrived.at[slot, t, pl.ds(s, half)]

            @pl.when(own)
            def _():
                pltpu.make_async_copy(src, dst, arrive_sem.at[slot, r]).start()

            @pl.when(jnp.logical_not(own))
            def _():
                pltpu.make_async_remote_copy(
                    src_ref=src,
                    dst_ref=dst,
                    send_sem=send_sem,
                    recv_sem=arrive_sem.at[slot, r],
                    device_id=device,
                    device_id_type=MESH,
                ).start()

            return 0

        lax.fori_loop(first, last, one, 0)

    def send_meta(i, _):
        own, device, _, slot = handler(i)

        @pl.when(own)
        def _():
            pltpu.make_async_copy(meta_vm, meta_in.at[slot], meta_sem.at[slot]).start()

        @pl.when(jnp.logical_not(own))
        def _():
            pltpu.make_async_remote_copy(
                src_ref=meta_vm,
                dst_ref=meta_in.at[slot],
                send_sem=meta_send,
                recv_sem=meta_sem.at[slot],
                device_id=device,
                device_id_type=MESH,
            ).start()

        return 0

    lax.fori_loop(0, 32, send_meta, 0)
    send_piece(0, 0, 8)
    send_piece(1, 0, 8)
    send_piece(2, 0, 8)
    send_piece(3, 0, 8)

    order = lax.broadcasted_iota(I32, (side, side), 0)
    source = lax.broadcasted_iota(I32, (side, side), 1)
    sort = (source == 2 * (order % (side // 2)) + order // (side // 2)).astype(BF16)
    zero = jnp.zeros((side, side), BF16)

    def prepare(n, _):
        f = fock_ref[n]
        top = jnp.concatenate([f, zero], axis=1)
        low = jnp.concatenate([zero, f], axis=1)
        fock_right[n] = jnp.concatenate([top, low], axis=0)
        g = jnp.dot(sort, f, preferred_element_type=F32).astype(BF16)
        g = lax.dot_general(g, sort, (((1,), (1,)), ((), ())), preferred_element_type=F32)
        fock_left[n] = g.astype(BF16)
        return 0

    lax.fori_loop(0, fock_ref.shape[0], prepare, 0)

    chunks = width // cols
    low_half = lax.broadcasted_iota(I32, (chunks, cols), 1) < side

    def residual(k, _):
        t, s = k // slots, k % slots
        pltpu.make_async_copy(amp_ref.at[t, s], amp_vm.at[k], amp_sem.at[k]).wait()
        ident = map_ref[owner_ref[t, s] * per_owner + local_ref[t, s]]
        used = counts_ref[t] > s
        row_tile = ident // fock_ref.shape[0]
        col_tile = ident % fock_ref.shape[0]
        for j in range(chunks):
            spread[pl.ds(j, rows, stride=chunks), :] = amp_vm[k, :, j * cols : (j + 1) * cols].astype(F32)
        for q in range(rows // 2):
            a = spread[2 * q * chunks : (2 * q + 1) * chunks, :]
            b = spread[(2 * q + 1) * chunks : (2 * q + 2) * chunks, :]
            even = jnp.where(low_half, a, pltpu.roll(b, side, 1))
            odd = jnp.where(low_half, pltpu.roll(a, side, 1), b)
            turned[:, q * cols : (q + 1) * cols] = jnp.concatenate([even, odd], axis=0).astype(BF16)
        left = jnp.dot(fock_left[row_tile], turned[...], preferred_element_type=F32)
        for q in range(rows // 2):
            even = left[:chunks, q * cols : (q + 1) * cols]
            odd = left[chunks:, q * cols : (q + 1) * cols]
            spread[2 * q * chunks : (2 * q + 1) * chunks, :] = jnp.where(
                low_half, even, pltpu.roll(odd, side, 1)
            )
            spread[(2 * q + 1) * chunks : (2 * q + 2) * chunks, :] = jnp.where(
                low_half, pltpu.roll(even, side, 1), odd
            )
        weight = hole_ref[t]
        right = fock_right[col_tile]
        for j in range(chunks):
            block = amp_vm[k, :, j * cols : (j + 1) * cols]
            total = jnp.dot(weight, block, preferred_element_type=F32)
            total += jnp.dot(block, right, preferred_element_type=F32)
            total += spread[pl.ds(j, rows, stride=chunks), :]
            res_ref[t, s, :, j * cols : (j + 1) * cols] = jnp.where(used, total, 0.0).astype(BF16)
        return 0

    lax.fori_loop(0, 4, residual, 0)
    third(0)
    for dw in (3, 1, 2):
        second(dw)
    send_piece(0, 8, 32)
    lax.fori_loop(4, 9, residual, 0)
    for dw in (3, 1, 2):
        third(dw)
    send_piece(1, 8, 32)
    lax.fori_loop(9, 13, residual, 0)
    send_piece(2, 8, 32)
    send_piece(3, 8, 32)
    lax.fori_loop(13, 16, residual, 0)
    all_panels()
    def wait_meta(slot, _):
        pltpu.make_async_copy(meta_vm, meta_in.at[slot], meta_sem.at[slot]).wait()
        return 0

    lax.fori_loop(0, 32, wait_meta, 0)
    pltpu.sync_copy(meta_in, meta_sm)

    def ladder(dw, t, first, last):
        group = dw * 8
        for r in range(first // half, last // half):

            def wait_slot(k, _, r=r):
                there = arrived.at[group + k, t, pl.ds(r * half, half)]
                pltpu.make_async_copy(there, there, arrive_sem.at[group + k, t * 2 + r]).wait()
                return 0

            lax.fori_loop(0, 8, wait_slot, 0)
        sums = []
        for k in range(8):
            blocks = [arrived[group + k, t, s] for s in range(first, last)]
            weights = [panels[meta_sm[group + k, c, t * slots + s]] for s in range(first, last)]
            sums.append(
                jnp.dot(
                    jnp.concatenate(blocks, axis=1),
                    jnp.concatenate(weights, axis=0),
                    preferred_element_type=F32,
                )
            )
        for k in range(8):
            if first == 0:
                part[t, group + k] = sums[k]
            else:
                part[t, group + k] += sums[k]

    def pass_sums(dw, t):
        pltpu.make_async_remote_copy(
            src_ref=part.at[t, pl.ds(dw * 8, 8)],
            dst_ref=part_in.at[t, dw - 1],
            send_sem=part_send,
            recv_sem=part_sem.at[t, dw - 1],
            device_id=at(x, ring(w, SIDE - dw), u, c),
            device_id_type=MESH,
        ).start()

    def part_of_list(t, first, last):
        def one(g, _):
            dw = pick(g, RINGS)
            ladder(dw, t, first, last)
            if last == slots:
                pl.when(dw > 0)(lambda: pass_sums(dw, t))
            return 0

        lax.fori_loop(0, SIDE, one, 0)

    def send_home(t):
        for dw in range(1, SIDE):
            there = part_in.at[t, dw - 1]
            pltpu.make_async_copy(there, there, part_sem.at[t, dw - 1]).wait()
        for k in (2, 3, 6, 7, 4, 5, 0, 1):
            dx, core = k // 2, k % 2
            ring_sum[t, k] = (
                part[t, k] + part_in[t, 0, k] + part_in[t, 1, k] + part_in[t, 2, k]
            )
            src, dst, sem = ring_sum.at[t, k], home_in.at[t, c, dx], home_sem.at[t, c, dx]

            def far(src=src, dst=dst, sem=sem, dx=dx, core=core):
                pltpu.make_async_remote_copy(
                    src_ref=src,
                    dst_ref=dst,
                    send_sem=home_send,
                    recv_sem=sem,
                    device_id=(occ, ring(x, SIDE - dx) * 2 + core),
                    device_id_type=MESH,
                ).start()

            if dx:
                far()
            else:
                pl.when(c != core)(far)

                @pl.when(c == core)
                def _(src=src, dst=dst, sem=sem):
                    pltpu.make_async_copy(src, dst, sem).start()

    def finish(t):
        total = jnp.zeros(lad_ref.shape[1:], F32)
        for h in range(2):
            for dx in range(SIDE):
                there = home_in.at[t, h, dx]
                pltpu.make_async_copy(there, there, home_sem.at[t, h, dx]).wait()
                total = total + home_in[t, h, dx]
        lad_ref[t] = total.astype(BF16)

    part_of_list(0, 0, slots)
    part_of_list(1, 0, half)
    send_home(0)
    part_of_list(1, half, slots)
    finish(0)
    send_home(1)
    finish(1)

    def drained(ref, sem):
        pltpu.make_async_copy(ref, ref, sem).wait()

    drained(amp_ref.at[:, :, :, pl.ds(0, width - cols)], send_sem)
    drained(meta_in.at[pl.ds(0, 31)], meta_send)
    drained(panels.at[pl.ds(0, 15 * per_owner)], panel_send)
    drained(part_in, part_send)
    drained(home_in.at[:, 0], home_send)
    drained(home_in.at[:, 0, pl.ds(0, 3)], home_send)


def per_device(
    amplitudes,
    tile_counts,
    tile_owner,
    tile_local,
    pair_map,
    hole_weight,
    fock_tiles,
    ladder_panels,
):
    tiles, slots, rows, width = amplitudes.shape
    per_owner, depth, panel = ladder_panels.shape
    tile_count, side, _ = fock_tiles.shape
    cols = 128
    dma = pltpu.SemaphoreType.DMA
    smem, vmem, hbm = (pl.BlockSpec(memory_space=m) for m in (pltpu.SMEM, pltpu.VMEM, pl.ANY))
    flops = 2 * tiles * slots * rows * width * (3 * side + panel)
    return pl.pallas_call(
        body,
        out_shape=(
            pltpu.VMEM(amplitudes.shape, BF16),
            jax.ShapeDtypeStruct((tiles, rows, panel), BF16),
        ),
        in_specs=[smem, smem, smem, smem, hbm, vmem, vmem, hbm],
        out_specs=(vmem, vmem),
        scratch_shapes=[
            pltpu.VMEM((tiles * slots, rows, width), BF16),
            pltpu.VMEM((32, tiles, slots, rows, cols), BF16),
            pltpu.VMEM((16 * per_owner + 1, cols, panel), BF16),
            pltpu.VMEM((8, 128), I32),
            pltpu.VMEM((32, 8, 128), I32),
            pltpu.SMEM((32, 8, 128), I32),
            pltpu.VMEM((tiles, 32, rows, panel), F32),
            pltpu.VMEM((tiles, 3, 8, rows, panel), F32),
            pltpu.VMEM((tiles, 8, rows, panel), F32),
            pltpu.VMEM((tiles, 2, SIDE, rows, panel), F32),
            pltpu.VMEM((tile_count, 2 * side, 2 * side), BF16),
            pltpu.VMEM((tile_count, side, side), BF16),
            pltpu.VMEM((rows * width // cols, cols), F32),
            pltpu.VMEM((side, rows * width // side), BF16),
            dma((tiles * slots,)),
            dma(()),
            dma((32, 4)),
            dma(()),
            dma((32,)),
            dma(()),
            dma(()),
            dma((SIDE,)),
            dma((SIDE, 2, 2)),
            dma((SIDE, 2)),
            dma(()),
            dma((tiles, 3)),
            dma(()),
            dma((tiles, 2, SIDE)),
        ],
        compiler_params=pltpu.CompilerParams(
            collective_id=0, has_side_effects=True, vmem_limit_bytes=54 << 20
        ),
        cost_estimate=pl.CostEstimate(
            flops=flops, bytes_accessed=4 * tiles * slots * rows * width, transcendentals=0
        ),
    )(
        tile_counts,
        tile_owner,
        tile_local,
        pair_map,
        amplitudes,
        hole_weight,
        fock_tiles,
        ladder_panels,
    )


def solution(mesh):
    in_specs = (
        P(("occ", "vir"), None, None, None),
        P(("occ", "vir")),
        P(("occ", "vir"), None),
        P(("occ", "vir"), None),
        P(),
        P(("occ", "vir"), None, None),
        P(),
        P("occ", "vir", None),
    )
    out_specs = (P(("occ", "vir"), None, None, None), P(("occ", "vir"), None, None))
    return jax.shard_map(
        per_device, mesh=mesh, in_specs=in_specs, out_specs=out_specs, check_vma=False
    )
```

```python
import functools

import jax
import jax.numpy as jnp
from jax import lax
from jax.experimental import pallas as pl
from jax.experimental.pallas import tpu as pltpu
from jax.sharding import PartitionSpec as P

MESH = pl.DeviceIdType.MESH
SIDE = 4
BF16, F32, I32 = jnp.bfloat16, jnp.float32, jnp.int32
HOPS = (1, 3, 2, 0)
RINGS = (0, 2, 1, 3)


def body(
    counts_ref,
    owner_ref,
    local_ref,
    map_ref,
    amp_ref,
    hole_ref,
    fock_ref,
    panel_ref,
    res_ref,
    lad_ref,
    amp_vm,
    arrived,
    panels,
    meta_vm,
    meta_in,
    meta_sm,
    part,
    part_in,
    ring_sum,
    home_in,
    direct_in,
    fock_right,
    fock_left,
    spread,
    turned,
    amp_sem,
    send_sem,
    arrive_sem,
    meta_send,
    meta_sem,
    panel_send,
    panel_own,
    panel_first,
    panel_second,
    panel_third,
    part_send,
    part_sem,
    home_send,
    home_sem,
    direct_sem,
):
    tiles, slots, rows, width = amp_ref.shape
    per_owner = panel_ref.shape[0]
    side = fock_ref.shape[1]
    cols = 128
    occ, vir = lax.axis_index("occ"), lax.axis_index("vir")
    y, z = occ // SIDE, occ % SIDE
    x, c = vir // 2, vir % 2
    w = jnp.where(c == 0, z, y)
    u = jnp.where(c == 0, y, z)

    def at(xx, ww, uu, core):
        own = jnp.where(core == 0, uu * SIDE + ww, ww * SIDE + uu)
        return (own, xx * 2 + core)

    def pick(k, table):
        return jnp.where(
            k == 0, table[0], jnp.where(k == 1, table[1], jnp.where(k == 2, table[2], table[3]))
        )

    def ring(v, d):
        return lax.rem(v + d + SIDE, SIDE)

    barrier = pltpu.get_barrier_semaphore()
    greeted = 0
    for dx in range(SIDE):
        for dw in range(SIDE):
            for dc in range(2):
                if (dx, dw, dc) != (0, 0, 0):
                    cc = lax.rem(c + dc, 2)
                    own = jnp.where(c == 0, u * SIDE + ring(w, dw), ring(w, dw) * SIDE + u)
                    pl.semaphore_signal(
                        barrier, inc=1, device_id=(own, ring(x, dx) * 2 + cc), device_id_type=MESH
                    )
                    greeted += 1
    for du in range(1, SIDE):
        pl.semaphore_signal(barrier, inc=1, device_id=at(x, w, ring(u, du), c), device_id_type=MESH)
        greeted += 1

    for dx in range(SIDE):
        far = jnp.where(c == 0, ring(y, 3) * SIDE + z, y * SIDE + ring(z, 3))
        pl.semaphore_signal(
            barrier, inc=1, device_id=(far, ring(x, dx) * 2 + 1 - c), device_id_type=MESH
        )
        greeted += 1

    for k in range(tiles * slots):
        pltpu.make_async_copy(
            amp_ref.at[k // slots, k % slots], amp_vm.at[k], amp_sem.at[k]
        ).start()
    lane = lax.broadcasted_iota(I32, (8, 128), 1)
    row = lax.broadcasted_iota(I32, (8, 128), 0)
    listed = jnp.zeros((8, 128), I32)
    for t in range(tiles):
        for s in range(slots):
            own, loc = owner_ref[t, s], local_ref[t, s]
            used = counts_ref[t] > s
            none = per_owner * SIDE * SIDE
            straight = jnp.where(used, own * per_owner + loc, none)
            crossed = jnp.where(
                used, ((own % SIDE) * SIDE + own // SIDE) * per_owner + loc, none
            )
            here = lane == t * slots + s
            listed = jnp.where(here & (row == 0), straight, listed)
            listed = jnp.where(here & (row == 1), crossed, listed)
    meta_vm[...] = listed
    panels[per_owner * SIDE * SIDE] = jnp.zeros((cols, panel_ref.shape[2]), BF16)

    pl.semaphore_wait(barrier, greeted)

    def my_rows(ww):
        return panel_ref.at[:, pl.ds(pl.multiple_of(ww * cols, cols), cols), :]

    def place(uu, ww):
        return panels.at[pl.ds((uu * SIDE + ww) * per_owner, per_owner)]

    own_panel = pltpu.make_async_copy(my_rows(w), place(u, w), panel_own)
    own_panel.start()
    for dw in (1, 3, 2):
        pltpu.make_async_remote_copy(
            src_ref=my_rows(ring(w, dw)),
            dst_ref=place(u, w),
            send_sem=panel_send,
            recv_sem=panel_first.at[dw],
            device_id=at(x, ring(w, dw), u, c),
            device_id_type=MESH,
        ).start()

    part_tiles = per_owner // 2

    def place_part(uu, ww, p):
        return panels.at[pl.ds((uu * SIDE + ww) * per_owner + p * part_tiles, part_tiles)]

    def pass_panels(dw, p, du):
        there = place_part(u, ring(w, dw), p)
        held = panel_ref.at[
            pl.ds(p * part_tiles, part_tiles), pl.ds(pl.multiple_of(w * cols, cols), cols), :
        ]
        pltpu.make_async_remote_copy(
            src_ref=there if dw else held,
            dst_ref=there,
            send_sem=panel_send,
            recv_sem=panel_second.at[dw, p, du // 2],
            device_id=at(x, w, ring(u, du), c),
            device_id_type=MESH,
        ).start()

    def wait_neighbour(dw, p, du):
        there = place_part(ring(u, SIDE - du), ring(w, dw), p)
        pltpu.make_async_copy(there, there, panel_second.at[dw, p, du // 2]).wait()

    def pass_on(dw, p):
        du = 1 if p == 0 else SIDE - 1
        there = place_part(ring(u, SIDE - du), ring(w, dw), p)
        pltpu.make_async_remote_copy(
            src_ref=there,
            dst_ref=there,
            send_sem=panel_send,
            recv_sem=panel_third.at[dw, p],
            device_id=at(x, w, ring(u, du), c),
            device_id_type=MESH,
        ).start()

    def wait_first(dw):
        there = place(u, ring(w, dw))
        pltpu.make_async_copy(there, there, panel_first.at[SIDE - dw]).wait()

    def second(dw):
        if dw:
            wait_first(dw)
        for p, du in ((0, 1), (1, 3), (1, 1), (0, 3)):
            pass_panels(dw, p, du)

    def third(dw):
        wait_neighbour(dw, 0, 1)
        pass_on(dw, 0)
        wait_neighbour(dw, 1, 3)
        pass_on(dw, 1)

    def all_panels():
        own_panel.wait()
        for dw in range(SIDE):
            wait_neighbour(dw, 1, 1)
            wait_neighbour(dw, 0, 3)
            for p in range(2):
                there = place_part(ring(u, 2), ring(w, dw), p)
                pltpu.make_async_copy(there, there, panel_third.at[dw, p]).wait()

    second(0)

    half = slots // 2

    def handler(i):
        dw, h, dx = pick(i // 8, RINGS), (i // 4) % 2, pick(i % 4, HOPS)
        xx = ring(x, dx)
        ww = ring(jnp.where(h == 0, z, y), dw)
        uu = jnp.where(h == 0, y, z)
        own = (dw == 0) & (dx == 0) & (h == c)
        col = (2 * xx + h) * (SIDE * cols) + ww * cols
        slot = (dw * SIDE + dx) * 2 + c
        return own, at(xx, ww, uu, h), col, slot

    def send_piece(r, first=0, last=32):
        t, s = r // 2, (r % 2) * half

        def one(i, _):
            own, device, col, slot = handler(i)
            src = amp_ref.at[t, pl.ds(s, half), :, pl.ds(pl.multiple_of(col, cols), cols)]
            dst = arrived.at[slot, t, pl.ds(s, half)]

            @pl.when(own)
            def _():
                pltpu.make_async_copy(src, dst, arrive_sem.at[slot, r]).start()

            @pl.when(jnp.logical_not(own))
            def _():
                pltpu.make_async_remote_copy(
                    src_ref=src,
                    dst_ref=dst,
                    send_sem=send_sem,
                    recv_sem=arrive_sem.at[slot, r],
                    device_id=device,
                    device_id_type=MESH,
                ).start()

            return 0

        lax.fori_loop(first, last, one, 0)

    def send_meta(i, _):
        own, device, _, slot = handler(i)

        @pl.when(own)
        def _():
            pltpu.make_async_copy(meta_vm, meta_in.at[slot], meta_sem.at[slot]).start()

        @pl.when(jnp.logical_not(own))
        def _():
            pltpu.make_async_remote_copy(
                src_ref=meta_vm,
                dst_ref=meta_in.at[slot],
                send_sem=meta_send,
                recv_sem=meta_sem.at[slot],
                device_id=device,
                device_id_type=MESH,
            ).start()

        return 0

    lax.fori_loop(0, 32, send_meta, 0)
    send_piece(0, 0, 8)
    send_piece(1, 0, 8)
    send_piece(2, 0, 8)
    send_piece(3, 0, 8)

    order = lax.broadcasted_iota(I32, (side, side), 0)
    source = lax.broadcasted_iota(I32, (side, side), 1)
    sort = (source == 2 * (order % (side // 2)) + order // (side // 2)).astype(BF16)
    zero = jnp.zeros((side, side), BF16)

    def prepare(n, _):
        f = fock_ref[n]
        top = jnp.concatenate([f, zero], axis=1)
        low = jnp.concatenate([zero, f], axis=1)
        fock_right[n] = jnp.concatenate([top, low], axis=0)
        g = jnp.dot(sort, f, preferred_element_type=F32).astype(BF16)
        g = lax.dot_general(g, sort, (((1,), (1,)), ((), ())), preferred_element_type=F32)
        fock_left[n] = g.astype(BF16)
        return 0

    lax.fori_loop(0, fock_ref.shape[0], prepare, 0)

    chunks = width // cols
    low_half = lax.broadcasted_iota(I32, (chunks, cols), 1) < side

    def residual(k, _):
        t, s = k // slots, k % slots
        pltpu.make_async_copy(amp_ref.at[t, s], amp_vm.at[k], amp_sem.at[k]).wait()
        ident = map_ref[owner_ref[t, s] * per_owner + local_ref[t, s]]
        used = counts_ref[t] > s
        row_tile = ident // fock_ref.shape[0]
        col_tile = ident % fock_ref.shape[0]
        for j in range(chunks):
            spread[pl.ds(j, rows, stride=chunks), :] = amp_vm[k, :, j * cols : (j + 1) * cols].astype(F32)
        for q in range(rows // 2):
            a = spread[2 * q * chunks : (2 * q + 1) * chunks, :]
            b = spread[(2 * q + 1) * chunks : (2 * q + 2) * chunks, :]
            even = jnp.where(low_half, a, pltpu.roll(b, side, 1))
            odd = jnp.where(low_half, pltpu.roll(a, side, 1), b)
            turned[:, q * cols : (q + 1) * cols] = jnp.concatenate([even, odd], axis=0).astype(BF16)
        left = jnp.dot(fock_left[row_tile], turned[...], preferred_element_type=F32)
        for q in range(rows // 2):
            even = left[:chunks, q * cols : (q + 1) * cols]
            odd = left[chunks:, q * cols : (q + 1) * cols]
            spread[2 * q * chunks : (2 * q + 1) * chunks, :] = jnp.where(
                low_half, even, pltpu.roll(odd, side, 1)
            )
            spread[(2 * q + 1) * chunks : (2 * q + 2) * chunks, :] = jnp.where(
                low_half, pltpu.roll(even, side, 1), odd
            )
        weight = hole_ref[t]
        right = fock_right[col_tile]
        for j in range(chunks):
            block = amp_vm[k, :, j * cols : (j + 1) * cols]
            total = jnp.dot(weight, block, preferred_element_type=F32)
            total += jnp.dot(block, right, preferred_element_type=F32)
            total += spread[pl.ds(j, rows, stride=chunks), :]
            res_ref[t, s, :, j * cols : (j + 1) * cols] = jnp.where(used, total, 0.0).astype(BF16)
        return 0

    lax.fori_loop(0, 4, residual, 0)
    third(0)
    for dw in (3, 1, 2):
        second(dw)
    send_piece(0, 8, 32)
    lax.fori_loop(4, 9, residual, 0)
    for dw in (3, 1, 2):
        third(dw)
    send_piece(1, 8, 32)
    lax.fori_loop(9, 13, residual, 0)
    send_piece(2, 8, 32)
    send_piece(3, 8, 32)
    lax.fori_loop(13, 16, residual, 0)
    all_panels()
    def wait_meta(slot, _):
        pltpu.make_async_copy(meta_vm, meta_in.at[slot], meta_sem.at[slot]).wait()
        return 0

    lax.fori_loop(0, 32, wait_meta, 0)
    pltpu.sync_copy(meta_in, meta_sm)

    def ladder(dw, t, first, last):
        group = dw * 8
        for r in range(first // half, last // half):

            def wait_slot(k, _, r=r):
                there = arrived.at[group + k, t, pl.ds(r * half, half)]
                pltpu.make_async_copy(there, there, arrive_sem.at[group + k, t * 2 + r]).wait()
                return 0

            lax.fori_loop(0, 8, wait_slot, 0)
        sums = []
        for k in range(8):
            blocks = [arrived[group + k, t, s] for s in range(first, last)]
            weights = [panels[meta_sm[group + k, c, t * slots + s]] for s in range(first, last)]
            sums.append(
                jnp.dot(
                    jnp.concatenate(blocks, axis=1),
                    jnp.concatenate(weights, axis=0),
                    preferred_element_type=F32,
                )
            )
        for k in range(8):
            if first == 0:
                part[t, group + k] = sums[k]
            else:
                part[t, group + k] += sums[k]

    def pass_sums(dw, t):
        pltpu.make_async_remote_copy(
            src_ref=part.at[t, pl.ds(dw * 8, 8)],
            dst_ref=part_in.at[t, dw - 1],
            send_sem=part_send,
            recv_sem=part_sem.at[t, dw - 1],
            device_id=at(x, ring(w, SIDE - dw), u, c),
            device_id_type=MESH,
        ).start()

    def part_of_list(t, first, last, groups=SIDE):
        def one(g, _):
            dw = pick(g, RINGS)
            ladder(dw, t, first, last)
            if last == slots:
                pl.when(dw > 0)(lambda: pass_sums(dw, t))
            return 0

        lax.fori_loop(0, groups, one, 0)

    def send_direct(t):
        for k in range(8):
            dx, core = k // 2, k % 2
            pltpu.make_async_remote_copy(
                src_ref=part.at[t, 24 + k],
                dst_ref=direct_in.at[c, dx],
                send_sem=part_send,
                recv_sem=direct_sem.at[c, dx],
                device_id=(at(x, ring(w, 1), u, c)[0], ring(x, SIDE - dx) * 2 + core),
                device_id_type=MESH,
            ).start()

    def send_home(t):
        for dw in range(1, SIDE if t == 0 else 3):
            there = part_in.at[t, dw - 1]
            pltpu.make_async_copy(there, there, part_sem.at[t, dw - 1]).wait()
        for k in (2, 3, 6, 7, 4, 5, 0, 1):
            dx, core = k // 2, k % 2
            total = part[t, k] + part_in[t, 0, k] + part_in[t, 1, k]
            ring_sum[t, k] = total + part_in[t, 2, k] if t == 0 else total
            src, dst, sem = ring_sum.at[t, k], home_in.at[t, c, dx], home_sem.at[t, c, dx]

            def far(src=src, dst=dst, sem=sem, dx=dx, core=core):
                pltpu.make_async_remote_copy(
                    src_ref=src,
                    dst_ref=dst,
                    send_sem=home_send,
                    recv_sem=sem,
                    device_id=(occ, ring(x, SIDE - dx) * 2 + core),
                    device_id_type=MESH,
                ).start()

            if dx:
                far()
            else:
                pl.when(c != core)(far)

                @pl.when(c == core)
                def _(src=src, dst=dst, sem=sem):
                    pltpu.make_async_copy(src, dst, sem).start()

    def finish(t):
        total = jnp.zeros(lad_ref.shape[1:], F32)
        for h in range(2):
            for dx in range(SIDE):
                there = home_in.at[t, h, dx]
                pltpu.make_async_copy(there, there, home_sem.at[t, h, dx]).wait()
                total = total + home_in[t, h, dx]
                if t == 1:
                    there = direct_in.at[h, dx]
                    pltpu.make_async_copy(there, there, direct_sem.at[h, dx]).wait()
                    total = total + direct_in[h, dx]
        lad_ref[t] = total.astype(BF16)

    part_of_list(0, 0, slots)
    part_of_list(1, 0, half)
    send_home(0)
    part_of_list(1, half, slots, SIDE - 1)
    finish(0)
    ladder(RINGS[3], 1, half, slots)
    send_direct(1)
    send_home(1)
    finish(1)

    def drained(ref, sem):
        pltpu.make_async_copy(ref, ref, sem).wait()

    drained(amp_ref.at[:, :, :, pl.ds(0, width - cols)], send_sem)
    drained(meta_in.at[pl.ds(0, 31)], meta_send)
    drained(panels.at[pl.ds(0, 15 * per_owner)], panel_send)
    drained(part_in, part_send)
    drained(home_in.at[:, 0], home_send)
    drained(home_in.at[:, 0, pl.ds(0, 3)], home_send)


def per_device(
    amplitudes,
    tile_counts,
    tile_owner,
    tile_local,
    pair_map,
    hole_weight,
    fock_tiles,
    ladder_panels,
):
    tiles, slots, rows, width = amplitudes.shape
    per_owner, depth, panel = ladder_panels.shape
    tile_count, side, _ = fock_tiles.shape
    cols = 128
    dma = pltpu.SemaphoreType.DMA
    smem, vmem, hbm = (pl.BlockSpec(memory_space=m) for m in (pltpu.SMEM, pltpu.VMEM, pl.ANY))
    flops = 2 * tiles * slots * rows * width * (3 * side + panel)
    return pl.pallas_call(
        body,
        out_shape=(
            pltpu.VMEM(amplitudes.shape, BF16),
            jax.ShapeDtypeStruct((tiles, rows, panel), BF16),
        ),
        in_specs=[smem, smem, smem, smem, hbm, vmem, vmem, hbm],
        out_specs=(vmem, vmem),
        scratch_shapes=[
            pltpu.VMEM((tiles * slots, rows, width), BF16),
            pltpu.VMEM((32, tiles, slots, rows, cols), BF16),
            pltpu.VMEM((16 * per_owner + 1, cols, panel), BF16),
            pltpu.VMEM((8, 128), I32),
            pltpu.VMEM((32, 8, 128), I32),
            pltpu.SMEM((32, 8, 128), I32),
            pltpu.VMEM((tiles, 32, rows, panel), F32),
            pltpu.VMEM((tiles, 3, 8, rows, panel), F32),
            pltpu.VMEM((tiles, 8, rows, panel), F32),
            pltpu.VMEM((tiles, 2, SIDE, rows, panel), F32),
            pltpu.VMEM((2, SIDE, rows, panel), F32),
            pltpu.VMEM((tile_count, 2 * side, 2 * side), BF16),
            pltpu.VMEM((tile_count, side, side), BF16),
            pltpu.VMEM((rows * width // cols, cols), F32),
            pltpu.VMEM((side, rows * width // side), BF16),
            dma((tiles * slots,)),
            dma(()),
            dma((32, 4)),
            dma(()),
            dma((32,)),
            dma(()),
            dma(()),
            dma((SIDE,)),
            dma((SIDE, 2, 2)),
            dma((SIDE, 2)),
            dma(()),
            dma((tiles, 3)),
            dma(()),
            dma((tiles, 2, SIDE)),
            dma((2, SIDE)),
        ],
        compiler_params=pltpu.CompilerParams(
            collective_id=0, has_side_effects=True, vmem_limit_bytes=54 << 20
        ),
        cost_estimate=pl.CostEstimate(
            flops=flops, bytes_accessed=4 * tiles * slots * rows * width, transcendentals=0
        ),
    )(
        tile_counts,
        tile_owner,
        tile_local,
        pair_map,
        amplitudes,
        hole_weight,
        fock_tiles,
        ladder_panels,
    )


def solution(mesh):
    in_specs = (
        P(("occ", "vir"), None, None, None),
        P(("occ", "vir")),
        P(("occ", "vir"), None),
        P(("occ", "vir"), None),
        P(),
        P(("occ", "vir"), None, None),
        P(),
        P("occ", "vir", None),
    )
    out_specs = (P(("occ", "vir"), None, None, None), P(("occ", "vir"), None, None))
    return jax.shard_map(
        per_device, mesh=mesh, in_specs=in_specs, out_specs=out_specs, check_vma=False
    )
```
